32 devices in a mesh: pipe: 2 (over core), dp: 16 (over z, y, x).
Axes of the slice: x: 2, y: 2, z: 4, core: 2. Of those that a mesh axis runs over, the one named last changes fastest.
Arguments:
- inputs: bfloat16 [2, 32, 512, 512], P('pipe', 'dp'), may hold values from -6 to 6
- src_len: int32 [32], P('dp'), may hold values from 128 to 512, as said below
- tgt_len: int32 [32], P('dp'), may hold values from 128 to 512, as said below
- groups: int32 [32], P('dp'), may hold values from 0 to 7
- cotangent: bfloat16 [2, 32, 512, 512], P('pipe', 'dp'), may hold values from -6 to 6
- attn_w: bfloat16 [2, 512, 2048], P('pipe'), as said below
- ffn_in: bfloat16 [2, 512, 2048], P('pipe'), may hold values from -0.25 to 0.25
- ffn_in_bias: bfloat16 [2, 2048], P('pipe'), may hold values from -3 to 3
- ffn_out: bfloat16 [2, 2048, 512], P('pipe'), may hold values from -0.125 to 0.125
- ffn_out_bias: bfloat16 [2, 512], P('pipe'), may hold values from -2 to 2
- norm_gain: bfloat16 [2, 2, 512], P('pipe'), may hold values from 0.5 to 1.5
- norm_bias: bfloat16 [2, 2, 512], P('pipe'), may hold values from -2 to 2
- cross_w: bfloat16 [512, 2048], P(None, 'pipe'), as said below
- cross_gain: bfloat16 [512], replicated, may hold values from 0.5 to 1.5
- cross_bias: bfloat16 [512], replicated, may hold values from -2 to 2
- pair_table: bfloat16 [8, 512], replicated, may hold values from -3 to 3
Outputs:
- outputs: float32 [2, 32, 512, 512], P('pipe', 'dp')
- input_grads: float32 [2, 32, 512, 512], P('pipe', 'dp')
- attn_w_grad: float32 [2, 512, 2048], P('pipe')
- ffn_in_grad: float32 [2, 512, 2048], P('pipe')
- ffn_in_bias_grad: float32 [2, 2048], P('pipe')
- ffn_out_grad: float32 [2, 2048, 512], P('pipe')
- ffn_out_bias_grad: float32 [2, 512], P('pipe')
- norm_gain_grad: float32 [2, 2, 512], P('pipe')
- norm_bias_grad: float32 [2, 2, 512], P('pipe')
- cross_w_grad: float32 [512, 2048], P(None, 'pipe')
- cross_gain_grad: float32 [512], replicated
- cross_bias_grad: float32 [512], replicated
- pair_table_grad: float32 [8, 512], replicated
The draws below stay inside these ranges and needn't reach their ends.
Inputs may be any that keep to these rules, and one draw needn't show every extreme that they name: `src_len`: each source length is a whole number; in every draw one pair has exactly 512 and one exactly a quarter of 512 live source positions. `tgt_len`: likewise for target lengths. `attn_w`: independent normal entries; in each section's block the last 512 columns have deviation 0.5, the others deviation 1 / sqrt(512). `cross_w`: independent normal entries; the last 512 columns have deviation 0.5, the others deviation 1 / sqrt(512).
All inputs are finite; a program needn't handle non-finite values.
Results may differ from the reference program's by a relative error of at most 0.013.
Values may be sent and summed in bfloat16 or wider, within the bound.
A program may use at most 256 MiB of HBM per device.

```python
import jax
import jax.numpy as jnp
from jax import lax

D = 512
HEADS = 8
FF = 2048
SEQ = 512
SEQ_DEV = 2
PAIRS = 8
BLOCK = 512
BATCH = 32
N_DP = 16


output_scale = 0.5


def ragged_lengths(key):
    first_key, second_key = jax.random.split(key)
    lengths = jax.random.randint(first_key, (BATCH,), SEQ // 4, SEQ + 1)
    chosen = jax.random.permutation(second_key, BATCH)
    lengths = lengths.at[chosen[0]].set(SEQ)
    lengths = lengths.at[chosen[1]].set(SEQ // 4)
    return lengths.astype(jnp.int32)


def draw_src_len(key, part):
    key = jax.random.fold_in(key, 11)
    return ragged_lengths(key)


def draw_tgt_len(key, part):
    key = jax.random.fold_in(key, 12)
    return ragged_lengths(key)


def scaled_projection(key, shape, last_columns):
    values = jax.random.normal(key, shape, jnp.float32)
    column = jnp.arange(shape[-1])
    factor = jnp.where(column < shape[-1] - last_columns, D ** (-0.5), output_scale)
    return values * factor


def draw_attn_w(key, part):
    key = jax.random.fold_in(key, 21)
    return scaled_projection(key, (2, D, 4 * D), D).astype(jnp.bfloat16)


def draw_cross_w(key, part):
    key = jax.random.fold_in(key, 22)
    return scaled_projection(key, (D, 4 * D), D).astype(jnp.bfloat16)


def place_ends(result, own_key, smallest, top_value):
    index_at = [jax.random.randint(jax.random.fold_in(own_key, axis), (), 0, length) for axis, length in enumerate(result.shape)]
    widest = result.shape.index(max(result.shape))
    beside = index_at[:widest] + [(index_at[widest] + 1) % result.shape[widest]] + index_at[widest + 1:]
    return result.at[tuple(index_at)].set(smallest).at[tuple(beside)].set(top_value)


def block_scale(rng, extent, pieces, low, high):
    gain = 1.0
    for dim, blocks in pieces:
        draws = jax.random.uniform(jax.random.fold_in(jax.random.fold_in(rng, 6), dim), (blocks,), jnp.float32, low / len(pieces), high / len(pieces))
        gain = gain * jnp.repeat(jnp.exp(draws), extent[dim] // blocks).reshape((-1,) + (1,) * (len(extent) - 1 - dim))
    return gain


def bell_draw(stream_key, dims, scale, bound, cuts=(), held_as=jnp.bfloat16):
    array = scale * jax.random.normal(stream_key, dims, jnp.float32)
    if cuts:
        array = array * block_scale(stream_key, dims, cuts, -0.22, 0.18)
    return jnp.clip(array, -bound, bound).astype(held_as)


def setup_inputs(seed: int = 0) -> dict:
    key_list = jax.random.split(jax.random.key(seed), 17)
    return {
        "inputs": bell_draw(key_list[0], (2, BATCH, SEQ, D), 1.0, 6.0, ((0, 2), (1, 16))),
        "src_len": draw_src_len(jax.random.fold_in(key_list[16], 71), 0),
        "tgt_len": draw_tgt_len(jax.random.fold_in(key_list[16], 71), 0),
        "groups": place_ends(jax.random.randint(key_list[3], (BATCH,), 0, PAIRS), jax.random.fold_in(key_list[3], 1), 0, PAIRS - 1).astype(jnp.int32),
        "cotangent": bell_draw(key_list[4], (2, BATCH, SEQ, D), 1.0, 6.0, ((0, 2), (1, 16))),
        "attn_w": draw_attn_w(jax.random.fold_in(key_list[16], 71), 0),
        "ffn_in": bell_draw(key_list[6], (2, D, FF), D ** -0.5, 0.25, ((0, 2),)),
        "ffn_in_bias": bell_draw(key_list[7], (2, FF), 0.5, 3.0, ((0, 2),)),
        "ffn_out": bell_draw(key_list[8], (2, FF, D), FF ** -0.5, 0.125, ((0, 2),)),
        "ffn_out_bias": bell_draw(key_list[9], (2, D), 0.3, 2.0, ((0, 2),)),
        "norm_gain": jnp.clip(1.0 + 0.1 * jax.random.normal(key_list[10], (2, 2, D), jnp.float32), 0.5, 1.5).astype(jnp.bfloat16),
        "norm_bias": bell_draw(key_list[11], (2, 2, D), 0.3, 2.0, ((0, 2),)),
        "cross_w": draw_cross_w(jax.random.fold_in(key_list[16], 71), 0),
        "cross_gain": jnp.clip(1.0 + 0.1 * jax.random.normal(key_list[13], (D,), jnp.float32), 0.5, 1.5).astype(jnp.bfloat16),
        "cross_bias": bell_draw(key_list[14], (D,), 0.3, 2.0),
        "pair_table": bell_draw(key_list[15], (PAIRS, D), 0.5, 3.0),
    }


@jax.custom_vjp
def low(v):
    return lax.optimization_barrier(v.astype(jnp.bfloat16)).astype(jnp.float32)

@jax.custom_vjp
def low_back(v):
    return v

def low_keep(v):
    return (low(v), None)

def low_pass(kept, grad):
    return (grad,)

def back_keep(v):
    return (v, None)

def back_low(kept, grad):
    return (low(grad),)
low.defvjp(low_keep, low_pass)
low_back.defvjp(back_keep, back_low)
highest = lax.Precision.HIGHEST
norm_epsilon = 1e-05
masked_score = -1e+30

def product(left, right):
    return jnp.dot(left, right, precision=highest, preferred_element_type=jnp.float32)

def layer_norm(values, gain_row, shift_row):
    centred = values - lax.optimization_barrier(jnp.mean(values, axis=-1, keepdims=True))
    variance = lax.optimization_barrier(jnp.mean(centred * centred, axis=-1, keepdims=True))
    return centred * lax.rsqrt(variance + norm_epsilon) * gain_row + shift_row

def gelu_exact(values):
    return 0.5 * values * (1.0 + jax.scipy.special.erf(values * 0.7071067811865476))

def attention(queries, key_rows, value_rows, key_live, causal):
    row_count = queries.shape[0]
    block_rows = min(BLOCK, row_count)
    block_count = row_count // block_rows
    head_dim = queries.shape[1] // HEADS
    key_heads = key_rows.reshape(-1, HEADS, head_dim)
    value_heads = value_rows.reshape(-1, HEADS, head_dim)
    key_index = jnp.arange(key_rows.shape[0], dtype=jnp.int32)

    def one_block(block_args):
        block_queries, first_row = block_args
        query_heads = block_queries.reshape(block_rows, HEADS, head_dim)
        scores = jnp.einsum('qhd,khd->hqk', query_heads, key_heads, precision=highest) * head_dim ** (-0.5)
        scores = low_back(scores)
        allowed = jnp.broadcast_to(key_live[None, :] > 0.5, (block_rows, key_rows.shape[0]))
        if causal:
            query_index = first_row + jnp.arange(block_rows, dtype=jnp.int32)
            allowed = allowed & (key_index[None, :] <= query_index[:, None])
        scores = jnp.where(allowed[None], scores, masked_score)
        row_max = lax.optimization_barrier(jnp.max(scores, axis=-1, keepdims=True))
        shifted = jnp.exp(scores - row_max)
        soft_weights = low(shifted / lax.optimization_barrier(jnp.sum(shifted, axis=-1, keepdims=True)))
        mixed_rows = jnp.einsum('hqk,khd->qhd', soft_weights, value_heads, precision=highest)
        return mixed_rows.reshape(block_rows, HEADS * head_dim)
    blocks = queries.reshape(block_count, block_rows, queries.shape[1])
    firsts = (jnp.arange(block_count, dtype=jnp.int32) * block_rows).astype(jnp.int32)
    joined = lax.map(jax.checkpoint(one_block), (blocks, firsts))
    return low_back(low(joined.reshape(row_count, queries.shape[1])))

def encode(source, live_row, section_params, cross_kv):
    attn_block, ffn_first, bias_first, ffn_second, bias_second, gains, shifts = section_params
    projected = low_back(low(product(low(source), attn_block[:, :3 * D])))
    mixed_rows = attention(projected[:, :D], projected[:, D:2 * D], projected[:, 2 * D:], live_row, False)
    added = low_back(product(mixed_rows, attn_block[:, 3 * D:]))
    first_norm = layer_norm(source + added, gains[0], shifts[0])
    inner = low_back(product(low(first_norm), ffn_first) + bias_first)
    branch = low_back(product(low(gelu_exact(inner)), ffn_second) + bias_second)
    memory = layer_norm(source + first_norm + branch, gains[1], shifts[1]) * live_row[:, None]
    memory_kv = low_back(low(product(low(memory), cross_kv)))
    return (memory, memory_kv)

def decode(target, live_row, source_live, memory_kv, section_params, cross_query, cross_out, cross_gain, cross_bias):
    attn_block, ffn_first, bias_first, ffn_second, bias_second, gains, shifts = section_params
    projected = low_back(low(product(low(target), attn_block[:, :3 * D])))
    mixed_rows = attention(projected[:, :D], projected[:, D:2 * D], projected[:, 2 * D:], live_row, True)
    added = low_back(product(mixed_rows, attn_block[:, 3 * D:]))
    first_norm = layer_norm(target + added, gains[0], shifts[0])
    query_rows = low_back(low(product(low(first_norm), cross_query)))
    cross_mixed = attention(query_rows, memory_kv[:, :D], memory_kv[:, D:], source_live, False)
    cross_added = low_back(product(cross_mixed, cross_out))
    second_norm = layer_norm(first_norm + cross_added, cross_gain, cross_bias)
    inner = low_back(product(low(second_norm), ffn_first) + bias_first)
    branch = low_back(product(low(gelu_exact(inner)), ffn_second) + bias_second)
    return layer_norm(target + second_norm + branch, gains[1], shifts[1]) * live_row[:, None]

def reference(inputs, src_len, tgt_len, groups, cotangent, attn_w, ffn_in, ffn_in_bias, ffn_out, ffn_out_bias, norm_gain, norm_bias, cross_w, cross_gain, cross_bias, pair_table):
    params = tuple((argument.astype(jnp.float32) for argument in (attn_w, ffn_in, ffn_in_bias, ffn_out, ffn_out_bias, norm_gain, norm_bias, cross_w, cross_gain, cross_bias, pair_table)))
    positions = jnp.arange(SEQ, dtype=jnp.int32)
    src_live = (positions[None, :] < src_len[:, None]).astype(jnp.float32)
    tgt_live = (positions[None, :] < tgt_len[:, None]).astype(jnp.float32)
    pair_onehot = (groups[:, None] == jnp.arange(PAIRS, dtype=jnp.int32)[None, :]).astype(jnp.float32)
    stacked_in = inputs.astype(jnp.float32)

    def forward(stacked, weights):
        attn_all, first_all, first_bias, second_all, second_bias, gains_all, shifts_all, cross_all, cross_gain_f, cross_bias_f, table = weights
        tags = product(pair_onehot, table)
        enc_params = (attn_all[0], first_all[0], first_bias[0], second_all[0], second_bias[0], gains_all[0], shifts_all[0])
        dec_params = (attn_all[1], first_all[1], first_bias[1], second_all[1], second_bias[1], gains_all[1], shifts_all[1])

        def one_pair(pair_args):
            source, target, source_live, target_live, tag_row = pair_args
            memory, memory_kv = encode(source + tag_row[None, :], source_live, enc_params, cross_all[:, :2 * D])
            decoded = decode(target + tag_row[None, :], target_live, source_live, memory_kv, dec_params, cross_all[:, 2 * D:3 * D], cross_all[:, 3 * D:], cross_gain_f, cross_bias_f)
            return (memory, decoded)

        def scan_step(carry, group_args):
            return (carry, jax.vmap(one_pair)(group_args))
        grouped = (stacked[0].reshape(N_DP, SEQ_DEV, SEQ, D), stacked[1].reshape(N_DP, SEQ_DEV, SEQ, D), src_live.reshape(N_DP, SEQ_DEV, SEQ), tgt_live.reshape(N_DP, SEQ_DEV, SEQ), tags.reshape(N_DP, SEQ_DEV, D))
        _, (memories, decoded_all) = lax.scan(scan_step, jnp.zeros((), jnp.float32), grouped)
        return jnp.stack([memories.reshape(BATCH, SEQ, D), decoded_all.reshape(BATCH, SEQ, D)])
    outputs, pullback = jax.vjp(forward, stacked_in, params)
    input_grads, param_grads = pullback(cotangent.astype(jnp.float32))
    return (outputs, input_grads, param_grads[0], param_grads[1], param_grads[2], param_grads[3], param_grads[4], param_grads[5], param_grads[6], param_grads[7], param_grads[8], param_grads[9], param_grads[10])
```

```python
import functools
import math

import jax
import jax.numpy as jnp
from jax import lax
from jax.experimental import pallas as pl
from jax.experimental.pallas import tpu as pltpu
from jax.sharding import PartitionSpec as P

HEADS = 8
MESH = pl.DeviceIdType.MESH
norm_epsilon = 1e-05
masked_score = -1e30


def product(left, right):
    return jnp.dot(left, right, preferred_element_type=jnp.float32)


def product_left(left, right):
    return lax.dot_general(
        left, right, (((0,), (0,)), ((), ())), preferred_element_type=jnp.float32
    )


def product_right(left, right):
    return lax.dot_general(
        left, right, (((1,), (1,)), ((), ())), preferred_element_type=jnp.float32
    )


def gelu_both(values):
    cumulative = 0.5 * (1.0 + lax.erf(values * 0.7071067811865476))
    density = jnp.exp(-0.5 * values * values) * 0.3989422804014327
    return values * cumulative, cumulative + values * density


def norm_forward(values, gain_row, shift_row):
    centred = values - jnp.mean(values, axis=-1, keepdims=True)
    inverse = lax.rsqrt(jnp.mean(centred * centred, axis=-1, keepdims=True) + norm_epsilon)
    normed = centred * inverse
    return (normed * gain_row + shift_row, (normed, inverse))


def norm_backward(grad_out, saved_norm, gain_row):
    normed, inverse = saved_norm
    grad_normed = grad_out * gain_row
    grad_in = inverse * (
        grad_normed
        - jnp.mean(grad_normed, axis=-1, keepdims=True)
        - normed * jnp.mean(grad_normed * normed, axis=-1, keepdims=True)
    )
    return (grad_in, jnp.sum(grad_out * normed, axis=0), jnp.sum(grad_out, axis=0))


def attend_forward(queries, key_rows, value_rows, allowed):
    rows, features = queries.shape
    head_dim = features // HEADS
    split = lambda v: v.reshape(-1, HEADS, head_dim)
    scores = jnp.einsum(
        "qhd,khd->hqk", split(queries), split(key_rows), preferred_element_type=jnp.float32
    ) * head_dim ** (-0.5)
    scores = jnp.where(allowed[None], scores, masked_score)
    row_max = jnp.max(scores, axis=-1, keepdims=True)
    shifted = jnp.exp(scores - row_max)
    row_total = jnp.sum(shifted, axis=-1, keepdims=True)
    weights = (shifted / row_total).astype(jnp.bfloat16)
    mixed = jnp.einsum("hqk,khd->qhd", weights, split(value_rows), preferred_element_type=jnp.float32)
    return mixed.reshape(rows, features).astype(jnp.bfloat16), row_max + jnp.log(row_total)


def attend_backward(queries, key_rows, value_rows, allowed, log_totals, grad_mixed):
    rows, features = queries.shape
    head_dim = features // HEADS
    scale = head_dim ** (-0.5)
    split = lambda v: v.reshape(-1, HEADS, head_dim)
    q, k, v, g = map(split, (queries, key_rows, value_rows, grad_mixed))
    scores = jnp.einsum("qhd,khd->hqk", q, k, preferred_element_type=jnp.float32) * scale
    weights = jnp.where(allowed[None], jnp.exp(scores - log_totals), 0.0)
    grad_values = jnp.einsum(
        "hqk,qhd->khd", weights.astype(jnp.bfloat16), g, preferred_element_type=jnp.float32
    )
    grad_weights = jnp.einsum("qhd,khd->hqk", g, v, preferred_element_type=jnp.float32)
    centre = jnp.sum(weights * grad_weights, axis=-1, keepdims=True)
    grad_scores = (weights * (grad_weights - centre)).astype(jnp.bfloat16)
    grad_query = jnp.einsum("hqk,khd->qhd", grad_scores, k, preferred_element_type=jnp.float32) * scale
    grad_keys = jnp.einsum("hqk,qhd->khd", grad_scores, q, preferred_element_type=jnp.float32) * scale
    flat = lambda t: t.reshape(-1, features)
    return flat(grad_query), flat(grad_keys), flat(grad_values)


def attention_forward(rows_round, attn_block, allowed):
    n = rows_round.shape[1]
    packed = product(rows_round, attn_block[:, : 3 * n]).astype(jnp.bfloat16)
    mixed, logs = attend_forward(packed[:, :n], packed[:, n : 2 * n], packed[:, 2 * n :], allowed)
    return product(mixed, attn_block[:, 3 * n :]), (packed, mixed, logs)


def attention_backward(grad_added, rows_round, attn_block, allowed, kept):
    packed, mixed, logs = kept
    n = rows_round.shape[1]
    grad_round = grad_added.astype(jnp.bfloat16)
    grad_out_weight = product_left(mixed, grad_round)
    grad_mixed = product_right(grad_round, attn_block[:, 3 * n :]).astype(jnp.bfloat16)
    parts = attend_backward(
        packed[:, :n], packed[:, n : 2 * n], packed[:, 2 * n :], allowed, logs, grad_mixed
    )
    grad_packed = jnp.concatenate(parts, axis=1).astype(jnp.bfloat16)
    grad_in_weight = product_left(rows_round, grad_packed)
    grad_rows = product_right(grad_packed, attn_block[:, : 3 * n])
    return grad_rows, jnp.concatenate([grad_in_weight, grad_out_weight], axis=1)


def ffn_forward(hidden_round, ffn_first, bias_first, ffn_second, bias_second):
    inner = product(hidden_round, ffn_first) + bias_first
    active, slope = gelu_both(inner)
    active = active.astype(jnp.bfloat16)
    return product(active, ffn_second) + bias_second, (slope, active)


def ffn_backward(grad_branch, hidden_round, ffn_first, ffn_second, kept):
    slope, active = kept
    grad_round = grad_branch.astype(jnp.bfloat16)
    grad_second = product_left(active, grad_round)
    grad_bias_second = jnp.sum(grad_round.astype(jnp.float32), axis=0)
    grad_inner = (product_right(grad_round, ffn_second) * slope).astype(jnp.bfloat16)
    grad_first = product_left(hidden_round, grad_inner)
    grad_bias_first = jnp.sum(grad_inner.astype(jnp.float32), axis=0)
    grad_hidden = product_right(grad_inner, ffn_first)
    return grad_hidden, (grad_first, grad_bias_first, grad_second, grad_bias_second)


def halvings(rows, cols, count):
    sizes = [(rows, cols)]
    for _ in range(count):
        r, c = sizes[-1]
        sizes.append((r // 2, c) if r >= 32 else (r, c // 2))
    return sizes


def piece_list(shapes, count):
    chunks = []
    for t, (rows, cols) in enumerate(shapes):
        if rows <= 512 and cols > 1024:
            chunks += [(t, 0, c, rows, 1024) for c in range(0, cols, 1024)]
        elif rows > 1024:
            chunks += [(t, r, 0, 1024, cols) for r in range(0, rows, 1024)]
        else:
            chunks += [(t, 0, 0, rows, cols)]
    return chunks


def reduce_kernel(shapes, bits, g0, g1, g2, g3, small_ref, o0, o1, o2, o3, small_out,
                  r_sem, land0, land1, land2, land3, recv0, recv1, recv2, recv3,
                  small_acc, small_land, core_send, core_recv, send_sem, recv_sem,
                  small_send, small_recv):
    del r_sem
    grads = (g0, g1, g2, g3)
    total = (o0, o1, o2, o3)
    land = (land0, land1, land2, land3)
    arrive = (recv0, recv1, recv2, recv3)
    core = lax.axis_index("pipe")
    me = lax.axis_index("dp")
    orders = ([0, 2, 1, 3] + list(range(4, bits)), [1, 2, 0, 3] + list(range(4, bits)))
    orders = [[b for b in order if b < bits] for order in orders]
    my_bit = [lax.rem(me // (1 << b), 2) for b in range(bits)]
    partner = [
        {"dp": me + (1 << b) * (1 - 2 * my_bit[b])} for b in range(bits)
    ] + [{"pipe": 1 - core}]

    barrier = pltpu.get_barrier_semaphore()
    for device in partner:
        pl.semaphore_signal(barrier, inc=1, device_id=device, device_id_type=MESH)
    pl.semaphore_wait(barrier, len(partner))

    def remote(src, dst, send, recv, device):
        return pltpu.make_async_remote_copy(
            src_ref=src, dst_ref=dst, send_sem=send, recv_sem=recv,
            device_id=device, device_id_type=MESH,
        )

    chunks = piece_list(shapes, bits)

    small_acc[0] = small_ref[...]

    def small_copy(i):
        return remote(
            small_acc.at[i], small_land.at[i], small_send.at[i], small_recv.at[i], partner[i]
        )

    small_copy(0).start()

    def core_copy(k):
        t, r, c, rows, cols = chunks[k]
        where = (pl.ds(r, rows), pl.ds(c, cols))
        return remote(
            grads[t].at[(1 - core,) + where], arrive[t].at[where],
            core_send.at[k], core_recv.at[k], partner[bits],
        )

    def region(k, q, step):
        t, r, c, rows, cols = chunks[k]
        cols //= 2
        c = c + q * cols
        sizes = halvings(rows, cols, bits)
        for s in range(step):
            b = my_bit[orders[q][s]]
            (r0, c0), (r1, c1) = sizes[s], sizes[s + 1]
            if r1 != r0:
                r = r + b * r1
            else:
                c = c + b * c1
        return r, c, sizes[step]

    def other_region(k, q, step):
        r, c, (r0, c0) = region(k, q, step)
        t, _, _, rows, cols = chunks[k]
        r1, c1 = halvings(rows, cols // 2, bits)[step + 1]
        b = 1 - my_bit[orders[q][step]]
        if r1 != r0:
            r = r + b * r1
        else:
            c = c + b * c1
        return r, c, (r1, c1)

    def view(ref, reg):
        r, c, (rows, cols) = reg
        if not isinstance(r, int):
            r = pl.multiple_of(r, 16)
        if not isinstance(c, int):
            c = pl.multiple_of(c, 128)
        return ref.at[pl.ds(r, rows), pl.ds(c, cols)]

    def landing(k, q, step):
        t, r, c, rows, cols = chunks[k]
        cols //= 2
        c = c + q * cols
        sizes = halvings(rows, cols, bits)
        for s in range(step):
            (r0, c0), (r1, c1) = sizes[s], sizes[s + 1]
            if r1 != r0:
                r += r1
            else:
                c += c1
        return r, c, sizes[step + 1]

    def scatter_copy(k, q, step):
        t = chunks[k][0]
        return remote(
            view(arrive[t], other_region(k, q, step)), view(land[t], landing(k, q, step)),
            send_sem.at[k, q, step], recv_sem.at[k, q, step], partner[orders[q][step]],
        )

    def gather_copy(k, q, step):
        t = chunks[k][0]
        mine = region(k, q, step + 1)
        return remote(
            view(total[t], mine), view(total[t], mine),
            send_sem.at[k, q, 2 * bits - 1 - step], recv_sem.at[k, q, 2 * bits - 1 - step],
            partner[orders[q][step]],
        )

    def advance(k, stage):
        t, r, c, rows, cols = chunks[k]
        if stage == 0:
            core_copy(k).wait()
            where = (slice(r, r + rows), slice(c, c + cols))
            own = grads[t][(core,) + where].astype(jnp.float32)
            arrive[t][where] = (own + arrive[t][where].astype(jnp.float32)).astype(jnp.bfloat16)
        elif stage <= bits:
            for q in range(2):
                scatter_copy(k, q, stage - 1).wait()
                reg = region(k, q, stage)
                lr, lc, (lrows, lcols) = landing(k, q, stage - 1)
                mine = view(arrive[t], reg)
                into = view(total[t], reg) if stage == bits else mine
                got = land[t][lr : lr + lrows, lc : lc + lcols].astype(jnp.float32)
                into[...] = (mine[...].astype(jnp.float32) + got).astype(jnp.bfloat16)
        else:
            for q in range(2):
                gather_copy(k, q, 2 * bits - stage).wait()
        if stage < bits:
            for q in range(2):
                scatter_copy(k, q, stage).start()
        elif stage < 2 * bits:
            for q in range(2):
                gather_copy(k, q, 2 * bits - 1 - stage).start()

    for k in range(len(chunks)):
        core_copy(k).start()
    count, stages = len(chunks), 2 * bits + 1
    for t in range(count + stages - 1):
        for k in range(min(t, count - 1), -1, -1):
            if 0 <= t - k < stages:
                advance(k, t - k)
        if t <= bits:
            small_copy(t).wait()
            small_acc[t + 1] = small_acc[t] + small_land[t]
            if t < bits:
                small_copy(t + 1).start()
    small_out[...] = small_acc[bits + 1]


def reduce_all(grads, small, bits):
    shapes = tuple(g.shape[1:] for g in grads)
    vmem = pl.BlockSpec(memory_space=pltpu.VMEM)
    chunks = len(piece_list(shapes, bits))
    dma = pltpu.SemaphoreType.DMA
    return pl.pallas_call(
        functools.partial(reduce_kernel, shapes, bits),
        out_shape=[jax.ShapeDtypeStruct(s, jnp.bfloat16) for s in shapes]
        + [jax.ShapeDtypeStruct(small.shape, jnp.float32)],
        in_specs=[vmem] * 5,
        out_specs=[vmem] * 5,
        scratch_shapes=[pltpu.SemaphoreType.REGULAR]
        + [pltpu.VMEM(s, jnp.bfloat16) for s in shapes]
        + [pltpu.VMEM(s, jnp.bfloat16) for s in shapes]
        + [
            pltpu.VMEM((bits + 2,) + small.shape, jnp.float32),
            pltpu.VMEM((bits + 1,) + small.shape, jnp.float32),
            dma((chunks,)), dma((chunks,)),
            dma((chunks, 2, 2 * bits)), dma((chunks, 2, 2 * bits)),
            dma((bits + 1,)), dma((bits + 1,)),
        ],
        compiler_params=pltpu.CompilerParams(
            collective_id=0, has_side_effects=True, vmem_limit_bytes=56 << 20
        ),
    )(*grads, small)


def body(bits, inputs, src_len, tgt_len, groups, cotangent, attn_w, ffn_in, ffn_in_bias,
         ffn_out, ffn_out_bias, norm_gain, norm_bias, cross_w, cross_gain, cross_bias, pair_table):
    core = lax.axis_index("pipe")
    swap = lambda v: lax.ppermute(v, "pipe", [(0, 1), (1, 0)])
    first = core == 0

    def both(mine):
        other = swap(mine)
        return jnp.where(first, mine, other), jnp.where(first, other, mine)

    def both_pairs(mine):
        keep = lax.dynamic_index_in_dim(mine, core, 0, keepdims=False)
        other = swap(lax.dynamic_index_in_dim(mine, 1 - core, 0, keepdims=False))
        return jnp.where(first, keep, other), jnp.where(first, other, keep)

    f32 = lambda v: v.astype(jnp.float32)
    source, target = both_pairs(inputs[0])
    grad_memory_out, grad_target_out = both_pairs(cotangent[0])
    attn = both(attn_w[0])
    first_w = both(ffn_in[0])
    second_w = both(ffn_out[0])
    cross = both(cross_w)
    bias_first = both(f32(ffn_in_bias[0]))
    bias_second = both(f32(ffn_out_bias[0]))
    gains = both(f32(norm_gain[0]))
    shifts = both(f32(norm_bias[0]))
    cross_gain, cross_bias = f32(cross_gain), f32(cross_bias)

    pick = lambda v: lax.dynamic_index_in_dim(v, core, 0, keepdims=False)
    seq = inputs.shape[2]
    n = inputs.shape[3]
    positions = jnp.arange(seq, dtype=jnp.int32)
    source_live = positions < pick(src_len)
    target_live = positions < pick(tgt_len)
    hot = (pick(groups) == jnp.arange(pair_table.shape[0], dtype=jnp.int32)).astype(jnp.float32)
    tag = product(hot.astype(jnp.bfloat16)[None], pair_table)
    source_ok = jnp.broadcast_to(source_live[None], (seq, seq))
    target_ok = target_live[None] & (positions[None] <= positions[:, None])
    source_live = f32(source_live)[:, None]
    target_live = f32(target_live)[:, None]

    enc_in = f32(source) + tag
    enc_round = enc_in.astype(jnp.bfloat16)
    added, enc_attn = attention_forward(enc_round, attn[0], source_ok)
    h1e, saved_e1 = norm_forward(enc_in + added, gains[0][0], shifts[0][0])
    h1e_round = h1e.astype(jnp.bfloat16)
    branch, enc_ffn = ffn_forward(h1e_round, first_w[0], bias_first[0], second_w[0], bias_second[0])
    final, saved_e2 = norm_forward(enc_in + h1e + branch, gains[0][1], shifts[0][1])
    memory = final * source_live
    memory_round = memory.astype(jnp.bfloat16)
    memory_kv = product(memory_round, cross[0]).astype(jnp.bfloat16)
    dec_in = f32(target) + tag
    dec_round = dec_in.astype(jnp.bfloat16)
    added, dec_attn = attention_forward(dec_round, attn[1], target_ok)
    h1, saved_d1 = norm_forward(dec_in + added, gains[1][0], shifts[1][0])
    h1_round = h1.astype(jnp.bfloat16)
    cquery = product(h1_round, cross[1][:, :n]).astype(jnp.bfloat16)
    cmixed, clogs = attend_forward(cquery, memory_kv[:, :n], memory_kv[:, n:], source_ok)
    h2, saved_d2 = norm_forward(h1 + product(cmixed, cross[1][:, n:]), cross_gain, cross_bias)
    h2_round = h2.astype(jnp.bfloat16)
    branch, dec_ffn = ffn_forward(h2_round, first_w[1], bias_first[1], second_w[1], bias_second[1])
    final, saved_d3 = norm_forward(dec_in + h2 + branch, gains[1][1], shifts[1][1])
    decoded = final * target_live
    dsum, dg_d1, dc_d1 = norm_backward(f32(grad_target_out) * target_live, saved_d3, gains[1][1])
    dh, dec_f = ffn_backward(dsum, h2_round, first_w[1], second_w[1], dec_ffn)
    dpre2, dg_c, dc_c = norm_backward(dsum + dh, saved_d2, cross_gain)
    da = dpre2.astype(jnp.bfloat16)
    g_cross_out = product_left(cmixed, da)
    dcmixed = product_right(da, cross[1][:, n:]).astype(jnp.bfloat16)
    dq, dk, dv = attend_backward(cquery, memory_kv[:, :n], memory_kv[:, n:], source_ok, clogs, dcmixed)
    dcquery = dq.astype(jnp.bfloat16)
    dkv = jnp.concatenate([dk, dv], axis=1).astype(jnp.bfloat16)
    g_cross_q = product_left(h1_round, dcquery)
    dpre1, dg_d0, dc_d0 = norm_backward(dpre2 + product_right(dcquery, cross[1][:, :n]), saved_d1, gains[1][0])
    drows, g_attn_d = attention_backward(dpre1, dec_round, attn[1], target_ok, dec_attn)
    dtarget = dsum + dpre1 + drows
    g_cross_kv = product_left(memory_round, dkv)
    dmem = (f32(grad_memory_out) + product_right(dkv, cross[0])) * source_live
    dsum, dg_e1, dc_e1 = norm_backward(dmem, saved_e2, gains[0][1])
    dh, enc_f = ffn_backward(dsum, h1e_round, first_w[0], second_w[0], enc_ffn)
    dpre1, dg_e0, dc_e0 = norm_backward(dsum + dh, saved_e1, gains[0][0])
    drows, g_attn_e = attention_backward(dpre1, enc_round, attn[0], source_ok, enc_attn)
    dsource = dsum + dpre1 + drows

    low = lambda *vs: jnp.stack([v.astype(jnp.bfloat16) for v in vs])
    grads = (
        low(enc_f[2], dec_f[2]),
        low(enc_f[0], dec_f[0]),
        low(g_cross_kv, jnp.concatenate([g_cross_q, g_cross_out], axis=1)),
        low(g_attn_e, g_attn_d),
    )
    pair_grad = hot[:, None] * jnp.sum(dsource + dtarget, axis=0)[None]
    wide = lambda v: v.reshape(-1, n)
    section_rows = [
        jnp.concatenate([wide(f[1]), wide(f[3]), wide(g0), wide(g1), wide(c0), wide(c1)])
        for f, g0, g1, c0, c1 in (
            (enc_f, dg_e0, dg_e1, dc_e0, dc_e1), (dec_f, dg_d0, dg_d1, dc_d0, dc_d1)
        )
    ]
    small = jnp.concatenate(section_rows + [wide(dg_c), wide(dc_c), pair_grad])
    used = small.shape[0]
    small = jnp.pad(small, ((0, -used % 8), (0, 0)))
    out_g, first_g, cross_g, attn_g, small = reduce_all(grads, small, bits)

    per = section_rows[0].shape[0]
    mine = lax.dynamic_slice_in_dim(small, core * per, per, 0)
    ff = per - 5
    shared = small[2 * per :]

    def own(enc, dec):
        keep = jnp.where(first, enc, dec)
        other = swap(jnp.where(first, dec, enc))
        return jnp.where(first, jnp.stack([keep, other]), jnp.stack([other, keep]))[None]

    return (
        own(memory, decoded), own(dsource, dtarget),
        f32(attn_g)[None], f32(first_g)[None], mine[:ff].reshape(1, -1), f32(out_g)[None],
        mine[ff : ff + 1], mine[ff + 1 : ff + 3][None], mine[ff + 3 : ff + 5][None],
        f32(cross_g), shared[0], shared[1], shared[2 : 2 + pair_table.shape[0]],
    )


def solution(mesh):
    bits = int(math.log2(mesh.shape["dp"]))
    return jax.shard_map(
        functools.partial(body, bits),
        mesh=mesh,
        in_specs=(
            P("pipe", "dp", None, None), P("dp"), P("dp"), P("dp"), P("pipe", "dp", None, None),
            P("pipe", None, None), P("pipe", None, None), P("pipe", None), P("pipe", None, None),
            P("pipe", None), P("pipe", None, None), P("pipe", None, None), P(None, "pipe"),
            P(), P(), P(),
        ),
        out_specs=(
            P("pipe", "dp", None, None), P("pipe", "dp", None, None), P("pipe", None, None),
            P("pipe", None, None), P("pipe", None), P("pipe", None, None), P("pipe", None),
            P("pipe", None, None), P("pipe", None, None), P(None, "pipe"), P(), P(), P(),
        ),
        check_vma=False,
    )
```
